256 devices in a mesh: row: 8 (over x, core), col: 32 (over z, y).
Axes of the slice: x: 4, y: 4, z: 8, core: 2. Of those that a mesh axis runs over, the one named last changes fastest.
Arguments:
- density: float32 [1024, 8, 128, 128], P(('row', 'col'))
- pattern: int32 [1024, 8], P(('row', 'col')), may hold values from -1 to 1023, as said below
- square_target: int32 [1024, 16], P(('row', 'col')), may hold values from -1 to 1023, as said below
- cube_target: int32 [1024, 24], P(('row', 'col')), may hold values from -1 to 1023, as said below
Outputs:
- squared: float32 [1024, 16, 128, 128], P(('row', 'col'))
- purified: float32 [1024, 24, 128, 128], P(('row', 'col'))
The draws below stay inside these ranges and needn't reach their ends.
Inputs may be any that keep to these rules, and one draw needn't show every extreme that they name: `pattern`: in each block row the live slots come first and slot 0 holds the row's own block column; live columns are distinct and lie within 4 of the row's index, counted around the ends; each row has 5 to 8 live slots, and some row has exactly 8, some exactly 5. `square_target`: as pattern, with columns within 8 of the row's index and 5 to 16 live slots, both reached. `cube_target`: as pattern, with columns within 12 of the row's index and 5 to 24 live slots, both reached.
All inputs are finite; a program needn't handle non-finite values.
Results may differ from the reference program's by a relative error of at most 0.0003.
Values sent between devices are 32-bit elements; how exact they have to be, the bound alone decides.
No kernel may reach another device: no remote copies, remote signals or barrier semaphores. Data moves between devices by JAX's collectives and lax.ppermute only.
A program may use at most 192 MiB of HBM per device.

```python
import jax
import jax.numpy as jnp
from jax import lax

BS = 128
H = 4
KP = 8
KS = 16
KC = 24
LEAST = 5
NB = 1024


def band_lists(key, band_half_width, slot_count, fewest):
    count_key, score_key, chosen_key, second_key = jax.random.split(key, 4)
    candidates = 2 * band_half_width + 1
    offsets = jnp.arange(candidates) - band_half_width
    ranking_scores = jax.random.randint(score_key, (NB, candidates), 0, 1 << 20) * 64 + jnp.arange(candidates)[None, :]
    ranking_scores = jnp.where(offsets[None, :] == 0, -1, ranking_scores)
    ranking = jnp.argsort(ranking_scores, axis=1)
    chosen = offsets[ranking[:, :slot_count]]
    counts = jax.random.randint(count_key, (NB,), fewest, slot_count + 1)
    row_ids = jnp.arange(NB)
    fullest = jax.random.randint(chosen_key, (), 0, NB)
    thinnest = (fullest + 1 + jax.random.randint(second_key, (), 0, NB - 1)) % NB
    counts = jnp.where(row_ids == fullest, slot_count, counts)
    counts = jnp.where(row_ids == thinnest, fewest, counts)
    columns = jnp.mod(row_ids[:, None] + chosen, NB)
    live_slots = jnp.arange(slot_count)[None, :] < counts[:, None]
    return jnp.where(live_slots, columns, -1).astype(jnp.int32)


def draw_density(key, part):
    key = jax.random.fold_in(key, 5)
    first_key = jax.random.fold_in(key, 0)
    block_shape = (NB, KP, BS, BS)
    values = jnp.clip(jax.random.normal(first_key, block_shape, jnp.float32), -5.0, 5.0)
    diagonal = (jnp.arange(KP) == 0).astype(jnp.float32)[None, :, None, None] * jnp.eye(BS, dtype=jnp.float32)[None, None, :, :]
    return (values * BS ** (-0.5) + 0.5 * diagonal).astype(jnp.float32)


def draw_pattern(key, part):
    key = jax.random.fold_in(key, 21)
    return band_lists(key, H, KP, LEAST)


def draw_square_target(key, part):
    key = jax.random.fold_in(key, 31)
    return band_lists(key, 2 * H, KS, LEAST)


def draw_cube_target(key, part):
    key = jax.random.fold_in(key, 41)
    return band_lists(key, 3 * H, KC, LEAST)


def setup_inputs(seed: int = 0) -> dict:
    key_of = jax.random.split(jax.random.key(seed), 5)
    return {
        "density": draw_density(jax.random.fold_in(key_of[4], 71), 0),
        "pattern": draw_pattern(jax.random.fold_in(key_of[4], 71), 0),
        "square_target": draw_square_target(jax.random.fold_in(key_of[4], 71), 0),
        "cube_target": draw_cube_target(jax.random.fold_in(key_of[4], 71), 0),
    }


EXACT_ARITHMETIC = lax.Precision.HIGHEST


def block_product(left_blocks, left_cols, right_blocks, right_column_ids, targets, row_base, row_total):
    def one_row(row_item):
        blocks, columns, target_row = row_item
        slot_rows = jnp.where(columns >= 0, jnp.mod(columns - row_base, row_total), 0)
        selected_entries = jnp.take(right_blocks, slot_rows, axis=0)
        picked_cols = jnp.take(right_column_ids, slot_rows, axis=0)
        block_products_list = jnp.einsum("sab,subc->suac", blocks, selected_entries, precision=EXACT_ARITHMETIC, preferred_element_type=jnp.float32)
        matching_entries = jnp.logical_and(picked_cols[None, :, :] == target_row[:, None, None], target_row[:, None, None] >= 0).astype(jnp.float32)
        return jnp.einsum("fpn,pngi->fgi", matching_entries, block_products_list, precision=EXACT_ARITHMETIC, preferred_element_type=jnp.float32)

    return lax.map(one_row, (left_blocks, left_cols, targets))


def combine(squared, square_target, cubed, cube_target):
    shared_slots = jnp.logical_and(cube_target[:, :, None] == square_target[:, None, :], cube_target[:, :, None] >= 0).astype(jnp.float32)
    carried = jnp.einsum("rts,rsab->rtab", shared_slots, squared, precision=EXACT_ARITHMETIC, preferred_element_type=jnp.float32)
    kept_slots = (cube_target >= 0).astype(jnp.float32)[:, :, None, None]
    return kept_slots * (3.0 * carried - 2.0 * cubed)


def reference(density, pattern, square_target, cube_target):
    live_slots = (pattern >= 0)[:, :, None, None]
    masked = jnp.where(live_slots, density, jnp.zeros_like(density))
    row_total = masked.shape[0]
    squared = block_product(masked, pattern, masked, pattern, square_target, 0, row_total)
    cubed = block_product(masked, pattern, squared, square_target, cube_target, 0, row_total)
    return squared, combine(squared, square_target, cubed, cube_target)
```

```python
import functools

import jax
import jax.numpy as jnp
from jax import lax
from jax.experimental import pallas as pl
from jax.experimental.pallas import tpu as pltpu
from jax.sharding import PartitionSpec as P

AXES = ("row", "col")
ROWS, KP, KS, KC, BS = 4, 8, 16, 24, 128
UNROLL = 4
GROUP = 2 * UNROLL
CAP = (192 * KP + GROUP, 96 * KP + GROUP, 128 * KP + GROUP, 96 * KP + GROUP)
OFF = (0, CAP[0], CAP[0] + CAP[1], CAP[0] + CAP[1] + CAP[2])
TOTAL = sum(CAP)
ZERO_P = 96
VMEM_LIMIT = 60 * 1024 * 1024


def shifted(x, distance):
    n = lax.axis_size(AXES)
    return lax.ppermute(x, AXES, [((i - distance) % n, i) for i in range(n)])


def list_kernel(total_rows, base_ref, pat_ref, sq_ref, cu_ref, lists_ref, counts_ref, carry_ref, pos_p, pos_s):
    wrap = total_rows - 1
    base = base_ref[0]

    def clear(ref, size):
        def step(i, _):
            for q in range(8):
                ref[i * 8 + q] = -1
            return 0

        lax.fori_loop(0, size // 8, step, 0)

    clear(pos_p, 20 * 16)
    clear(pos_s, 12 * 32)

    def place_p(r, _):
        for u in range(KP):
            col = pat_ref[r * KP + u]

            @pl.when(col >= 0)
            def _():
                pos_p[r * 16 + jnp.minimum((col - base - r + 4) & wrap, 15)] = u

        return 0

    lax.fori_loop(0, 20, place_p, 0)

    def place_s(r, _):
        for u in range(KS):
            col = sq_ref[r * KS + u]

            @pl.when(col >= 0)
            def _():
                pos_s[r * 32 + jnp.minimum((col - base - 4 - r + 8) & wrap, 31)] = u

        return 0

    lax.fori_loop(0, 12, place_s, 0)

    def filler(zero_right):
        return ZERO_P | (zero_right << 8)

    def even(p, off, zero_right):
        lists_ref[off + p] = filler(zero_right)
        return p + (p & 1)

    def square_target(idx, carry):
        k = idx // KS
        col = sq_ref[idx]
        pa, pb = carry
        live = col >= 0
        for s in range(KP):
            m = pat_ref[(k + 4) * KP + s]
            mloc = jnp.minimum((m - base) & wrap, 19)
            u = pos_p[mloc * 16 + jnp.minimum((col - m + 4) & wrap, 15)]
            hit = jnp.logical_and(jnp.logical_and(live, m >= 0), u >= 0)
            near = jnp.logical_and(mloc >= 4, mloc < 16)
            left = (k * KP + s) | (idx << 16)
            lists_ref[OFF[0] + pa] = left | (((mloc - 4) * KP + u) << 8)
            far = jnp.where(mloc < 4, mloc, mloc - 12)
            lists_ref[OFF[2] + pb] = left | ((far * KP + u) << 8)
            pa = pa + jnp.where(jnp.logical_and(hit, near), 1, 0)
            pb = pb + jnp.where(jnp.logical_and(hit, jnp.logical_not(near)), 1, 0)
        return even(pa, OFF[0], 96), even(pb, OFF[2], 64)

    na, nc = lax.fori_loop(0, 12 * KS, square_target, (jnp.int32(0), jnp.int32(0)))

    def cube_target(idx, carry):
        i = idx // KC
        col = cu_ref[idx]
        pa, pb = carry
        live = col >= 0
        for s in range(KP):
            k = pat_ref[(i + 8) * KP + s]
            kloc = jnp.minimum((k - base - 4) & wrap, 11)
            u = pos_s[kloc * 32 + jnp.minimum((col - k + 8) & wrap, 31)]
            hit = jnp.logical_and(jnp.logical_and(live, k >= 0), u >= 0)
            near = jnp.logical_and(kloc >= 4, kloc < 8)
            left = ((i + 4) * KP + s) | (idx << 16)
            lists_ref[OFF[1] + pa] = left | (((kloc - 4) * KS + u) << 8)
            far = jnp.where(kloc < 4, kloc, kloc - 4)
            lists_ref[OFF[3] + pb] = left | ((far * KS + u) << 8)
            pa = pa + jnp.where(jnp.logical_and(hit, near), 1, 0)
            pb = pb + jnp.where(jnp.logical_and(hit, jnp.logical_not(near)), 1, 0)
        u = pos_s[(i + 4) * 32 + jnp.minimum((col - base - 8 - i + 8) & wrap, 31)]
        carry_ref[idx] = jnp.where(jnp.logical_and(live, u >= 0), i * KS + u, 64)
        return even(pa, OFF[1], 64), even(pb, OFF[3], 128)

    nb, nd = lax.fori_loop(0, 4 * KC, cube_target, (jnp.int32(0), jnp.int32(0)))

    for which, (n, zero_right) in enumerate(((na, 96), (nb, 64), (nc, 64), (nd, 128))):
        for q in range(GROUP):
            lists_ref[OFF[which] + n + q] = filler(zero_right)
        counts_ref[which] = (n + GROUP - 1) // GROUP


def pair_lists(base, pat20, sq12, cu4, total_rows):
    smem = pl.BlockSpec(memory_space=pltpu.SMEM)
    return pl.pallas_call(
        functools.partial(list_kernel, total_rows),
        out_shape=(
            jax.ShapeDtypeStruct((TOTAL,), jnp.int32),
            jax.ShapeDtypeStruct((4,), jnp.int32),
            jax.ShapeDtypeStruct((4 * KC,), jnp.int32),
        ),
        in_specs=[smem] * 4,
        out_specs=(smem,) * 3,
        scratch_shapes=[pltpu.SMEM((20 * 16,), jnp.int32), pltpu.SMEM((12 * 32,), jnp.int32)],
        cost_estimate=pl.CostEstimate(flops=20_000_000, bytes_accessed=40_000_000, transcendentals=0),
        name="pair_lists",
    )(base, pat20, sq12, cu4)


def halves(x):
    hi = x.astype(jnp.bfloat16)
    lo = (x - hi.astype(jnp.float32)).astype(jnp.bfloat16)
    return hi, lo


def put_left(ref, at, hi, lo):
    ref[at, 0:BS, :] = hi
    ref[at, BS : 2 * BS, :] = lo


def put_right(ref, at, hi, lo):
    ref[at, :, 0:BS] = hi
    ref[at, :, BS : 2 * BS] = lo


def multiply(lists_ref, off, groups, left, right, total):
    def group(g, _):
        at = off + g * GROUP
        done = []
        for x in range(UNROLL):
            e, f = lists_ref[at + 2 * x], lists_ref[at + 2 * x + 1]
            lhs = jnp.concatenate([left[e & 255], left[f & 255]], axis=1)
            rhs = jnp.concatenate([right[(e >> 8) & 255], right[(f >> 8) & 255]], axis=0)
            r = jnp.dot(lhs, rhs, preferred_element_type=jnp.float32)
            done.append((e >> 16, (r[:BS, :BS] + r[:BS, BS:]) + (r[BS:, :BS] + r[BS:, BS:])))
        for t, q in done:
            total[t] = total[t] + q
        return 0

    lax.fori_loop(0, groups, group, 0)


def near_kernel(lists, counts, below, own, above, s_out, sp_out, c_out, left_out, right, total, s_right):
    zero_l = jnp.zeros((2 * BS, BS), jnp.bfloat16)
    zero_r = jnp.zeros((BS, 2 * BS), jnp.bfloat16)
    left_out[ZERO_P] = zero_l
    right[96] = zero_r
    s_right[64] = zero_r
    for part, src in enumerate((below, own, above)):

        def cut(q, _):
            hi, lo = halves(src[q // KP, q % KP])
            put_left(left_out, part * 32 + q, hi, lo)
            put_right(right, part * 32 + q, hi, lo)
            return 0

        lax.fori_loop(0, 32, cut, 0)

    def clear(ref, n):
        def step(q, _):
            ref[q] = jnp.zeros((BS, BS), jnp.float32)
            return 0

        lax.fori_loop(0, n, step, 0)

    clear(total, 192)
    clear(c_out, 96)
    multiply(lists, OFF[0], counts[0], left_out, right, total)

    def share(q, _):
        x = total[64 + q]
        s_out[q] = x
        hi, lo = halves(x)
        put_right(s_right, q, hi, lo)
        sp_out[q] = total[q]
        sp_out[64 + q] = total[128 + q]
        return 0

    lax.fori_loop(0, 64, share, 0)
    multiply(lists, OFF[1], counts[1], left_out, s_right, c_out)


def near_step(lists, counts, below, own, above):
    smem = pl.BlockSpec(memory_space=pltpu.SMEM)
    vmem = pl.BlockSpec(memory_space=pltpu.VMEM)
    return pl.pallas_call(
        near_kernel,
        out_shape=(
            jax.ShapeDtypeStruct((64, BS, BS), jnp.float32),
            jax.ShapeDtypeStruct((128, BS, BS), jnp.float32),
            jax.ShapeDtypeStruct((96, BS, BS), jnp.float32),
            jax.ShapeDtypeStruct((97, 2 * BS, BS), jnp.bfloat16),
        ),
        in_specs=[smem, smem, vmem, vmem, vmem],
        out_specs=(vmem,) * 4,
        scratch_shapes=[
            pltpu.VMEM((97, BS, 2 * BS), jnp.bfloat16),
            pltpu.VMEM((192, BS, BS), jnp.float32),
            pltpu.VMEM((65, BS, 2 * BS), jnp.bfloat16),
        ],
        compiler_params=pltpu.CompilerParams(vmem_limit_bytes=VMEM_LIMIT),
        cost_estimate=pl.CostEstimate(flops=8_000_000_000, bytes_accessed=60_000_000, transcendentals=0),
        name="near_step",
    )(lists, counts, below, own, above)


def far_kernel(lists, counts, carry, below, above, left, sp, c_in, s_own, out, right, s_right):
    zero_r = jnp.zeros((BS, 2 * BS), jnp.bfloat16)
    right[64] = zero_r
    s_right[128] = zero_r
    for part, src in enumerate((below, above)):

        def cut(q, _):
            hi, lo = halves(src[q // KP, q % KP])
            put_right(right, part * 32 + q, hi, lo)
            return 0

        lax.fori_loop(0, 32, cut, 0)

    def far_total(t):
        return jnp.where(t >= 128, t - 64, t)

    def group(g, _):
        at = OFF[2] + g * GROUP
        done = []
        for x in range(UNROLL):
            e, f = lists[at + 2 * x], lists[at + 2 * x + 1]
            lhs = jnp.concatenate([left[e & 255], left[f & 255]], axis=1)
            rhs = jnp.concatenate([right[(e >> 8) & 255], right[(f >> 8) & 255]], axis=0)
            r = jnp.dot(lhs, rhs, preferred_element_type=jnp.float32)
            done.append((far_total(e >> 16), (r[:BS, :BS] + r[:BS, BS:]) + (r[BS:, :BS] + r[BS:, BS:])))
        for t, q in done:
            sp[t] = sp[t] + q
        return 0

    lax.fori_loop(0, counts[2], group, 0)

    def share(q, _):
        hi, lo = halves(sp[q])
        put_right(s_right, q, hi, lo)
        return 0

    lax.fori_loop(0, 128, share, 0)
    multiply(lists, OFF[3], counts[3], left, s_right, c_in)

    def finish(q, _):
        at = carry[q]
        kept = jnp.where(at < 64, 3.0, 0.0)
        out[q] = kept * s_own[jnp.minimum(at, 63)] - 2.0 * c_in[q]
        return 0

    lax.fori_loop(0, 96, finish, 0)


def far_step(lists, counts, carry, below, above, left, sp, c_in, s_own):
    smem = pl.BlockSpec(memory_space=pltpu.SMEM)
    vmem = pl.BlockSpec(memory_space=pltpu.VMEM)
    return pl.pallas_call(
        far_kernel,
        out_shape=jax.ShapeDtypeStruct((96, BS, BS), jnp.float32),
        in_specs=[smem] * 3 + [vmem] * 6,
        out_specs=vmem,
        scratch_shapes=[
            pltpu.VMEM((65, BS, 2 * BS), jnp.bfloat16),
            pltpu.VMEM((129, BS, 2 * BS), jnp.bfloat16),
        ],
        compiler_params=pltpu.CompilerParams(vmem_limit_bytes=VMEM_LIMIT),
        cost_estimate=pl.CostEstimate(flops=8_000_000_000, bytes_accessed=60_000_000, transcendentals=0),
        name="far_step",
    )(lists, counts, carry, below, above, left, sp, c_in, s_own)


def local(density, pattern, square_target, cube_target):
    total_rows = ROWS * lax.axis_size(AXES)
    first_row = lax.axis_index(AXES) * ROWS
    base = jnp.remainder(first_row - 2 * ROWS, total_rows).astype(jnp.int32).reshape(1)

    cols = jnp.concatenate([pattern, square_target], axis=1)
    m1, p1, m2, p2 = (shifted(cols, d) for d in (1, -1, 2, -2))
    density, m1, p1, m2, p2 = lax.optimization_barrier((density, m1, p1, m2, p2))
    below = shifted(density, 1)
    above = shifted(density, -1)
    pat20 = jnp.concatenate([m2[:, :KP], m1[:, :KP], pattern, p1[:, :KP], p2[:, :KP]], axis=0).reshape(-1)
    sq12 = jnp.concatenate([m1[:, KP:], square_target, p1[:, KP:]], axis=0).reshape(-1)
    lists, counts, carry = pair_lists(base, pat20, sq12, cube_target.reshape(-1), total_rows)
    below, above, lists, counts, carry = lax.optimization_barrier((below, above, lists, counts, carry))
    below2 = shifted(below, 1)
    above2 = shifted(above, -1)
    s_own, sp, c_part, left = near_step(lists, counts, below, density, above)
    out = far_step(lists, counts, carry, below2, above2, left, sp, c_part, s_own)
    return s_own.reshape(ROWS, KS, BS, BS), out.reshape(ROWS, KC, BS, BS)


def solution(mesh):
    in_specs = (P(AXES, None, None, None), P(AXES, None), P(AXES, None), P(AXES, None))
    out_specs = (P(AXES, None, None, None), P(AXES, None, None, None))
    return jax.shard_map(local, mesh=mesh, in_specs=in_specs, out_specs=out_specs, check_vma=False)
```

```python
import functools

import jax
import jax.numpy as jnp
import numpy as np
from jax import lax
from jax.experimental import pallas as pl
from jax.experimental.pallas import tpu as pltpu
from jax.sharding import PartitionSpec as P

AXES = ("row", "col")
ROWS, KP, KS, KC, BS = 4, 8, 16, 24, 128
HALF = ROWS // 2
PIECE = HALF * KP
UNROLL = 8
GROUP = 2 * UNROLL
ZERO_LEFT = 12 * KP

OWN, MIDDLE, LAST = (4, 5, 6, 7), (2, 3, 8, 9), (0, 1, 10, 11)
ORDER = OWN + MIDDLE + LAST

TARGETS = (12 * KS, 4 * KC, 8 * KS, 4 * KC, 4 * KS, 4 * KC)
ZERO_RIGHT = (12 * KP, 4 * KS, 2 * PIECE, 4 * KS, 2 * PIECE, 4 * KS)
TABLE_OFF = tuple(int(x) for x in np.cumsum((0,) + tuple(t * KP for t in TARGETS)))
LIST_OFF = tuple(int(x) for x in np.cumsum((0,) + tuple(t * KP + GROUP for t in TARGETS)))


def shifted(x, distance):
    n = lax.axis_size(AXES)
    return lax.ppermute(x, AXES, [((i - distance) % n, i) for i in range(n)])


def lookup(rows, count):
    table = np.full((count,), -1, np.int32)
    table[list(rows)] = np.arange(len(rows))
    return table


def pair_tables(base, pat20, sq12, cu4, total_rows):
    def place(cols, start, count):
        return jnp.minimum(jnp.remainder(cols - start, total_rows), count - 1)

    def matched(left_cols, right_cols, targets):
        same = right_cols[:, None, :, :] == targets[:, :, None, None]
        same = same & (targets >= 0)[:, :, None, None] & (left_cols >= 0)[:, None, :, None]
        return jnp.max(jnp.where(same, jnp.arange(right_cols.shape[-1], dtype=jnp.int32), -1), axis=-1)

    def pick(table, index):
        hot = index[..., None] == jnp.arange(table.shape[0], dtype=jnp.int32)
        shape = hot.shape + (1,) * (table.ndim - 1)
        return jnp.sum(jnp.where(hot.reshape(shape), table, 0), axis=index.ndim)

    def entries(u, left, right_row, width, target):
        right = right_row[:, None, :] * width + u
        ok = (u >= 0) & (right_row >= 0)[:, None, :]
        return jnp.where(ok, left[:, None, :] | (right << 8) | (target[:, :, None] << 16), -1).reshape(-1, KP)

    def const(x):
        return jnp.asarray(np.asarray(x, np.int32))

    slots = np.arange(KP, dtype=np.int32)
    near_p = lookup(range(4, 16), 20)
    mid_p = lookup((2, 3, 16, 17), 20)
    last_p = lookup((0, 1, 18, 19), 20)

    pk = pat20[4:16]
    at = place(pk, base, 20)
    u = matched(pk, pick(pat20, at), sq12)
    left = const(np.arange(12)[:, None] * KP + slots)
    tables = {}
    for which, (rows, here) in enumerate(((ORDER, near_p), (MIDDLE + LAST, mid_p), (LAST, last_p))):
        sel = np.asarray(rows)
        target = const(np.arange(len(rows))[:, None] * KS + np.arange(KS))
        take = lambda x: jnp.stack([x[r] for r in rows])
        tables[2 * which] = entries(take(u), const(np.arange(12)[sel][:, None] * KP + slots), pick(const(here), take(at)), KP, target)

    pi = pat20[8:12]
    at = place(pi, base + 4, 12)
    u = matched(pi, pick(sq12, at), cu4)
    left = const((np.arange(4) + 4)[:, None] * KP + slots)
    target = const(np.arange(4)[:, None] * KC + np.arange(KC))
    for which, rows in enumerate((OWN, MIDDLE, LAST)):
        tables[2 * which + 1] = entries(u, left, pick(const(lookup(rows, 12)), at), KS, target)

    same = (cu4[:, :, None] == sq12[4:8][:, None, :]) & (cu4 >= 0)[:, :, None]
    slot = jnp.max(jnp.where(same, jnp.arange(KS, dtype=jnp.int32), -1), axis=-1)
    carry = jnp.where(slot >= 0, slot + const(np.arange(4)[:, None] * KS), -1).reshape(-1)
    table = jnp.concatenate([tables[i] for i in range(6)])
    hit = table >= 0
    rank = jnp.sum(jnp.where(hit[:, None, :] & (slots[None, :] < slots[:, None])[None], 1, 0), axis=-1)
    moved = hit[:, None, :] & (rank[:, None, :] == slots[None, :, None])
    filler = const(np.repeat([ZERO_LEFT | (z << 8) for z in ZERO_RIGHT], TARGETS))[:, None]
    packed = jnp.where(jnp.any(moved, axis=-1), jnp.sum(jnp.where(moved, table[:, None, :], 0), axis=-1), filler)
    return packed.reshape(-1), jnp.sum(hit.astype(jnp.int32), axis=-1), carry


def list_kernel(table, hits, lists, counts):
    start = 0
    for which in range(6):
        t0, l0 = TABLE_OFF[which], LIST_OFF[which]

        def target(i, n):
            at = t0 + i * KP
            h = hits[start + i]
            lists[l0 + n] = table[at]
            lists[l0 + n + 1] = table[at + 1]

            @pl.when(h > 2)
            def _():
                for s in range(2, KP):
                    lists[l0 + n + s] = table[at + s]

            return n + ((h + 1) & 14)

        n = lax.fori_loop(0, TARGETS[which], target, jnp.int32(0))
        start += TARGETS[which]
        filler = ZERO_LEFT | (ZERO_RIGHT[which] << 8)
        for q in range(GROUP):
            lists[l0 + n + q] = filler
        counts[which] = (n + GROUP - 1) // GROUP


def pair_lists(table, hits):
    smem = pl.BlockSpec(memory_space=pltpu.SMEM)
    return pl.pallas_call(
        list_kernel,
        out_shape=(
            jax.ShapeDtypeStruct((LIST_OFF[-1],), jnp.int32),
            jax.ShapeDtypeStruct((6,), jnp.int32),
        ),
        in_specs=[smem, smem],
        out_specs=(smem, smem),
        cost_estimate=pl.CostEstimate(flops=20_000_000, bytes_accessed=40_000_000, transcendentals=0),
        name="pair_lists",
    )(table, hits)


def halves(x):
    hi = x.astype(jnp.bfloat16)
    lo = (x - hi.astype(jnp.float32)).astype(jnp.bfloat16)
    return hi, lo


def put_left(ref, at, hi, lo):
    ref[at, 0:BS, :] = hi
    ref[at, BS : 2 * BS, :] = lo


def put_right(ref, at, hi, lo):
    ref[at, :, 0:BS] = hi
    ref[at, :, BS : 2 * BS] = lo


def each(lo, hi, body, step=4):
    def many(i, _):
        for q in range(step):
            body(lo + i * step + q)
        return 0

    lax.fori_loop(0, (hi - lo) // step, many, 0)


def multiply(which, lists, counts, left, right, total):
    def group(g, _):
        at = LIST_OFF[which] + g * GROUP
        done = []
        for x in range(UNROLL):
            e, f = lists[at + 2 * x], lists[at + 2 * x + 1]
            lhs = jnp.concatenate([left[e & 255], left[f & 255]], axis=1)
            rhs = jnp.concatenate([right[(e >> 8) & 255], right[(f >> 8) & 255]], axis=0)
            r = jnp.dot(lhs, rhs, preferred_element_type=jnp.float32)
            done.append((e >> 16, (r[:BS, :BS] + r[:BS, BS:]) + (r[BS:, :BS] + r[BS:, BS:])))
        for t, q in done:
            total[t] = total[t] + q
        return 0

    lax.fori_loop(0, counts[which], group, 0)


def zero_left(left):
    left[ZERO_LEFT] = jnp.zeros((2 * BS, BS), jnp.bfloat16)


def zero_right(right, which):
    right[ZERO_RIGHT[which]] = jnp.zeros((BS, 2 * BS), jnp.bfloat16)


def near_kernel(
    lists, counts, carry, b1, a1, own, a2, b2, s_out, sp_out, c_out, left_out, stage, left, right, total, s_right, c, sems
):
    loads, at = [], 0
    for i, (src, n) in enumerate(((b1, PIECE), (a1, PIECE), (own, 2 * PIECE), (a2, PIECE), (b2, PIECE))):
        loads.append((pltpu.make_async_copy(src, stage.at[pl.ds(at, n)], sems.at[i]), at, n))
        at += n
    for copy, _, _ in loads:
        copy.start()
    zero_left(left)
    zero_right(right, 0)
    zero_right(s_right, 1)

    def clear(q):
        total[q] = jnp.zeros((BS, BS), jnp.float32)

    each(0, 12 * KS, clear)
    for copy, at, n in loads:
        copy.wait()

        def cut(q):
            hi, lo = halves(stage[q])
            put_left(left, q, hi, lo)
            put_right(right, q, hi, lo)

        each(at, at + n, cut)
    left_copy = pltpu.make_async_copy(left, left_out, sems.at[5])
    left_copy.start()
    multiply(0, lists, counts, left, right, total)
    s_copy = pltpu.make_async_copy(total.at[pl.ds(0, 4 * KS)], s_out, sems.at[6])
    sp_copy = pltpu.make_async_copy(total.at[pl.ds(4 * KS, 8 * KS)], sp_out, sems.at[7])
    s_copy.start()
    sp_copy.start()

    def share(q):
        hi, lo = halves(total[q])
        put_right(s_right, q, hi, lo)

    each(0, 4 * KS, share)

    def begin(q):
        at = carry[q]
        kept = jnp.where(at >= 0, -1.5, 0.0)
        c[q] = kept * total[jnp.maximum(at, 0)]

    each(0, 4 * KC, begin)
    multiply(1, lists, counts, left, s_right, c)
    c_copy = pltpu.make_async_copy(c, c_out, sems.at[8])
    c_copy.start()
    for copy in (left_copy, s_copy, sp_copy, c_copy):
        copy.wait()


def far_kernel(final, lists, counts, below, above, left_in, sp_in, c_in, *refs):
    if final:
        out, stage, left, right, total, s_right, c, sems = refs
    else:
        sp_out, out, stage, left, right, total, s_right, c, sems = refs
    which = 4 if final else 2
    p_copies = (
        pltpu.make_async_copy(below, stage.at[pl.ds(0, PIECE)], sems.at[0]),
        pltpu.make_async_copy(above, stage.at[pl.ds(PIECE, PIECE)], sems.at[1]),
    )
    left_copy = pltpu.make_async_copy(left_in, left, sems.at[2])
    sp_copy = pltpu.make_async_copy(sp_in, total, sems.at[3])
    c_copy = pltpu.make_async_copy(c_in, c, sems.at[4])
    for copy in p_copies + (left_copy, sp_copy, c_copy):
        copy.start()
    zero_right(right, which)
    zero_right(s_right, which + 1)
    for i, copy in enumerate(p_copies):
        copy.wait()

        def cut(q):
            hi, lo = halves(stage[q])
            put_right(right, q, hi, lo)

        each(i * PIECE, (i + 1) * PIECE, cut)
    left_copy.wait()
    sp_copy.wait()
    multiply(which, lists, counts, left, right, total)
    if not final:
        rest = pltpu.make_async_copy(total.at[pl.ds(4 * KS, 4 * KS)], sp_out, sems.at[5])
        rest.start()

    def share(q):
        hi, lo = halves(total[q])
        put_right(s_right, q, hi, lo)

    each(0, 4 * KS, share)
    c_copy.wait()
    multiply(which + 1, lists, counts, left, s_right, c)
    if not final:
        done = pltpu.make_async_copy(c, out, sems.at[6])
        done.start()
        rest.wait()
        done.wait()
        return
    done = []
    for i in range(ROWS):

        def finish(q):
            c[q] = -2.0 * c[q]

        each(i * KC, (i + 1) * KC, finish)
        piece = pl.ds(i * KC, KC)
        done.append(pltpu.make_async_copy(c.at[piece], out.at[piece], sems.at[5 + i]))
        done[-1].start()
    for copy in done:
        copy.wait()


SMEM = pl.BlockSpec(memory_space=pltpu.SMEM)
ANY = pl.BlockSpec(memory_space=pl.ANY)


def f32(n):
    return jax.ShapeDtypeStruct((n, BS, BS), jnp.float32)


def vmem_left():
    return pltpu.VMEM((ZERO_LEFT + 1, 2 * BS, BS), jnp.bfloat16)


def vmem_right(which):
    return pltpu.VMEM((ZERO_RIGHT[which] + 1, BS, 2 * BS), jnp.bfloat16)


def vmem_f32(n):
    return pltpu.VMEM((n, BS, BS), jnp.float32)


def near_step(lists, counts, carry, pieces):
    return pl.pallas_call(
        near_kernel,
        out_shape=(f32(4 * KS), f32(8 * KS), f32(4 * KC), jax.ShapeDtypeStruct((ZERO_LEFT + 1, 2 * BS, BS), jnp.bfloat16)),
        in_specs=[SMEM] * 3 + [ANY] * 5,
        out_specs=(ANY,) * 4,
        scratch_shapes=[
            vmem_f32(12 * KP),
            vmem_left(),
            vmem_right(0),
            vmem_f32(12 * KS),
            vmem_right(1),
            vmem_f32(4 * KC),
            pltpu.SemaphoreType.DMA((9,)),
        ],
        compiler_params=pltpu.CompilerParams(vmem_limit_bytes=48 * 1024 * 1024),
        cost_estimate=pl.CostEstimate(flops=20_000_000_000, bytes_accessed=60_000_000, transcendentals=0),
        name="near_step",
    )(lists, counts, carry, *pieces)


def far_step(final, lists, counts, below, above, left, sp, c):
    rows = 4 if final else 8
    out_shape = f32(4 * KC) if final else (f32(4 * KS), f32(4 * KC))
    return pl.pallas_call(
        functools.partial(far_kernel, final),
        out_shape=out_shape,
        in_specs=[SMEM] * 2 + [ANY] * 5,
        out_specs=ANY if final else (ANY, ANY),
        scratch_shapes=[
            vmem_f32(2 * PIECE),
            vmem_left(),
            vmem_right(2),
            vmem_f32(rows * KS),
            vmem_right(3),
            vmem_f32(4 * KC),
            pltpu.SemaphoreType.DMA((9,)),
        ],
        compiler_params=pltpu.CompilerParams(vmem_limit_bytes=36 * 1024 * 1024),
        cost_estimate=pl.CostEstimate(flops=10_000_000_000, bytes_accessed=40_000_000, transcendentals=0),
        name="last_step" if final else "middle_step",
    )(lists, counts, below, above, left, sp, c)


def local(density, pattern, square_target, cube_target):
    total_rows = ROWS * lax.axis_size(AXES)
    first_row = lax.axis_index(AXES) * ROWS
    base = jnp.remainder(first_row - 2 * ROWS, total_rows).astype(jnp.int32)
    hold = lax.optimization_barrier

    cols = jnp.concatenate([pattern, square_target], axis=1)
    cols_from = [shifted(cols, d) for d in (2, 1, -1, -2)]
    a1 = shifted(density[HALF:].reshape(PIECE, BS, BS), 1)
    a2 = shifted(density[:HALF].reshape(PIECE, BS, BS), -1)
    second, pattern, square_target, cube_target, *cols_from = hold(
        (density, pattern, square_target, cube_target, *cols_from)
    )
    b1 = shifted(second[:HALF].reshape(PIECE, BS, BS), 1)
    b2 = shifted(second[HALF:].reshape(PIECE, BS, BS), -1)
    near = jnp.concatenate(cols_from[:2] + [jnp.concatenate([pattern, square_target], axis=1)] + cols_from[2:], axis=0)
    table, hits, carry = pair_tables(base, near[:, :KP], near[4:16, KP:], cube_target, total_rows)
    a1, a2, table, hits, carry = hold((a1, a2, table, hits, carry))
    c1, c2 = shifted(a1, 1), shifted(a2, -1)
    lists, counts = pair_lists(table, hits)
    b1, b2, lists, counts, carry = hold((b1, b2, lists, counts, carry))
    d1, d2 = shifted(b1, 1), shifted(b2, -1)

    own = density.reshape(2 * PIECE, BS, BS)
    s_own, sp, c, left = near_step(lists, counts, carry, (b1, a1, own, a2, b2))
    sp, c = far_step(False, lists, counts, c1, c2, left, sp, c)
    out = far_step(True, lists, counts, d1, d2, left, sp, c)
    return s_own.reshape(ROWS, KS, BS, BS), out.reshape(ROWS, KC, BS, BS)


def solution(mesh):
    in_specs = (P(AXES, None, None, None), P(AXES, None), P(AXES, None), P(AXES, None))
    out_specs = (P(AXES, None, None, None), P(AXES, None, None, None))
    return jax.shard_map(local, mesh=mesh, in_specs=in_specs, out_specs=out_specs, check_vma=False)
```

```python
import functools

import jax
import jax.numpy as jnp
import numpy as np
from jax import lax
from jax.experimental import pallas as pl
from jax.experimental.pallas import tpu as pltpu
from jax.sharding import PartitionSpec as P

AXES = ("row", "col")
ROWS, KP, KS, KC, BS = 4, 8, 16, 24, 128
HALF = ROWS // 2
PIECE = HALF * KP
GROUP = 16
ZERO_LEFT = 12 * KP

OWN, MIDDLE, LAST = (4, 5, 6, 7), (2, 3, 8, 9), (0, 1, 10, 11)
ORDER = OWN + MIDDLE + LAST

TARGETS = (12 * KS, 4 * KC, 8 * KS, 4 * KC, 4 * KS, 4 * KC)
ZERO_RIGHT = (12 * KP, 4 * KS, 2 * PIECE, 4 * KS, 2 * PIECE, 4 * KS)
TABLE_OFF = tuple(int(x) for x in np.cumsum((0,) + tuple(t * KP for t in TARGETS)))
LIST_OFF = tuple(int(x) for x in np.cumsum((0,) + tuple(t * KP + GROUP for t in TARGETS)))


def shifted(x, distance):
    n = lax.axis_size(AXES)
    return lax.ppermute(x, AXES, [((i - distance) % n, i) for i in range(n)])


def lookup(rows, count):
    table = np.full((count,), -1, np.int32)
    table[list(rows)] = np.arange(len(rows))
    return table


def pair_tables(base, pat20, sq12, cu4, total_rows):
    def place(cols, start, count):
        return jnp.minimum(jnp.remainder(cols - start, total_rows), count - 1)

    def matched(left_cols, right_cols, targets):
        same = right_cols[:, None, :, :] == targets[:, :, None, None]
        same = same & (targets >= 0)[:, :, None, None] & (left_cols >= 0)[:, None, :, None]
        return jnp.max(jnp.where(same, jnp.arange(right_cols.shape[-1], dtype=jnp.int32), -1), axis=-1)

    def pick(table, index):
        hot = index[..., None] == jnp.arange(table.shape[0], dtype=jnp.int32)
        shape = hot.shape + (1,) * (table.ndim - 1)
        return jnp.sum(jnp.where(hot.reshape(shape), table, 0), axis=index.ndim)

    def entries(u, left, right_row, width, target):
        right = right_row[:, None, :] * width + u
        ok = (u >= 0) & (right_row >= 0)[:, None, :]
        return jnp.where(ok, left[:, None, :] | (right << 8) | (target[:, :, None] << 16), -1).reshape(-1, KP)

    def const(x):
        return jnp.asarray(np.asarray(x, np.int32))

    slots = np.arange(KP, dtype=np.int32)
    near_p = lookup(range(4, 16), 20)
    mid_p = lookup((2, 3, 16, 17), 20)
    last_p = lookup((0, 1, 18, 19), 20)

    pk = pat20[4:16]
    at = place(pk, base, 20)
    u = matched(pk, pick(pat20, at), sq12)
    pi = pat20[8:12]
    pi_at = place(pi, base + 4, 12)
    in_pattern = jnp.any((pi_at[:, :, None] == const(np.arange(12))) & (pi >= 0)[:, :, None], axis=1)
    in_cube = jnp.any(sq12[None, :, :, None] == cu4[:, None, None, :], axis=-1)
    used = jnp.any(in_pattern[:, :, None] & in_cube, axis=0) | const(lookup(OWN, 12) >= 0).astype(bool)[:, None]
    u = jnp.where(used[:, :, None], u, -1)
    tables = {}
    for which, (rows, here) in enumerate(((ORDER, near_p), (MIDDLE + LAST, mid_p), (LAST, last_p))):
        sel = np.asarray(rows)
        target = const(np.arange(len(rows))[:, None] * KS + np.arange(KS))
        take = lambda x: jnp.stack([x[r] for r in rows])
        tables[2 * which] = entries(take(u), const(np.arange(12)[sel][:, None] * KP + slots), pick(const(here), take(at)), KP, target)

    at = pi_at
    u = matched(pi, pick(sq12, at), cu4)
    left = const((np.arange(4) + 4)[:, None] * KP + slots)
    target = const(np.arange(4)[:, None] * KC + np.arange(KC))
    for which, rows in enumerate((OWN, MIDDLE, LAST)):
        tables[2 * which + 1] = entries(u, left, pick(const(lookup(rows, 12)), at), KS, target)

    same = (cu4[:, :, None] == sq12[4:8][:, None, :]) & (cu4 >= 0)[:, :, None]
    slot = jnp.max(jnp.where(same, jnp.arange(KS, dtype=jnp.int32), -1), axis=-1)
    carry = jnp.where(slot >= 0, slot + const(np.arange(4)[:, None] * KS), -1).reshape(-1)
    table = jnp.concatenate([tables[i] for i in range(6)])
    hit = table >= 0
    rank = jnp.sum(jnp.where(hit[:, None, :] & (slots[None, :] < slots[:, None])[None], 1, 0), axis=-1)
    moved = hit[:, None, :] & (rank[:, None, :] == slots[None, :, None])
    packed = jnp.sum(jnp.where(moved, table[:, None, :], 0), axis=-1)
    return packed.reshape(-1), jnp.sum(hit.astype(jnp.int32), axis=-1), carry


def list_kernel(table, hits, lists, counts):
    start = 0
    for which in range(6):
        t0, l0 = TABLE_OFF[which], LIST_OFF[which]

        def targets(i, n):
            first = i * 4
            h = [hits[start + first + q] for q in range(4)]
            at = [n]
            for q in range(4):
                at.append(at[-1] + h[q])
            e = [[table[t0 + (first + q) * KP + s] for s in range(4)] for q in range(4)]
            for q in range(4):
                for s in range(4):
                    lists[l0 + at[q] + s] = e[q][s]

                @pl.when(h[q] > 4)
                def _():
                    for s in range(4, KP):
                        lists[l0 + at[q] + s] = table[t0 + (first + q) * KP + s]

            return at[4]

        n = lax.fori_loop(0, TARGETS[which] // 4, targets, jnp.int32(0))
        start += TARGETS[which]
        filler = ZERO_LEFT | (ZERO_RIGHT[which] << 8)
        for q in range(GROUP):
            lists[l0 + n + q] = filler
        counts[which] = (n + GROUP - 1) // GROUP


def pair_lists(table, hits):
    smem = pl.BlockSpec(memory_space=pltpu.SMEM)
    return pl.pallas_call(
        list_kernel,
        out_shape=(
            jax.ShapeDtypeStruct((LIST_OFF[-1],), jnp.int32),
            jax.ShapeDtypeStruct((6,), jnp.int32),
        ),
        in_specs=[smem, smem],
        out_specs=(smem, smem),
        cost_estimate=pl.CostEstimate(flops=20_000_000, bytes_accessed=40_000_000, transcendentals=0),
        name="pair_lists",
    )(table, hits)


def halves(x):
    hi = x.astype(jnp.bfloat16)
    lo = (x - hi.astype(jnp.float32)).astype(jnp.bfloat16)
    return hi, lo


def put(ref, at, x):
    hi, lo = halves(x)
    ref[at, :, 0:BS] = hi
    ref[at, :, BS : 2 * BS] = lo


def each(lo, hi, body, step=4):
    def many(i, _):
        for q in range(step):
            body(lo + i * step + q)
        return 0

    lax.fori_loop(0, (hi - lo) // step, many, 0)


def multiply(which, lists, counts, left, right, total, scale=None):
    def group(g, _):
        at = LIST_OFF[which] + g * GROUP
        none = jnp.zeros((BS, BS), jnp.bfloat16)
        done = []
        for x in range(GROUP):
            e = lists[at + x]
            b = right[(e >> 8) & 255]
            rhs = jnp.concatenate([b, jnp.concatenate([b[:, :BS], none], axis=1)], axis=0)
            r = jnp.dot(left[e & 255], rhs, preferred_element_type=jnp.float32)
            done.append((e >> 16, r[:, :BS] + r[:, BS:]))
        for t, q in done:
            total[t] = total[t] + (q if scale is None else scale * q)
        return 0

    lax.fori_loop(0, counts[which], group, 0)


def zero(ref, at):
    ref[at] = jnp.zeros((BS, 2 * BS), jnp.bfloat16)


def near_kernel(lists, counts, carry, b1, a1, own, a2, b2, s_out, sp_out, c_out, cut_out, stage, cut, total, s_cut, c, sems):
    loads = []
    for i, (src, at, n) in enumerate(
        ((own, 2, 2), (a1, 1, 1), (a2, 4, 1), (b1, 0, 1), (b2, 5, 1))
    ):
        at, n = at * PIECE, n * PIECE
        loads.append((pltpu.make_async_copy(src, stage.at[pl.ds(at, n)], sems.at[i]), at, n))
    for copy, _, _ in loads:
        copy.start()
    zero(cut, ZERO_LEFT)
    zero(s_cut, 4 * KS)

    def clear(q):
        total[q] = jnp.zeros((BS, BS), jnp.float32)

    each(0, 12 * KS, clear)
    for copy, at, n in loads:
        copy.wait()
        each(at, at + n, lambda q: put(cut, q, stage[q]))
    cut_copy = pltpu.make_async_copy(cut, cut_out, sems.at[5])
    cut_copy.start()
    multiply(0, lists, counts, cut, cut, total)
    s_copy = pltpu.make_async_copy(total.at[pl.ds(0, 4 * KS)], s_out, sems.at[6])
    sp_copy = pltpu.make_async_copy(total.at[pl.ds(4 * KS, 8 * KS)], sp_out, sems.at[7])
    s_copy.start()
    sp_copy.start()
    each(0, 4 * KS, lambda q: put(s_cut, q, total[q]))

    def begin(q):
        at = carry[q]
        kept = jnp.where(at >= 0, -1.5, 0.0)
        c[q] = kept * total[jnp.maximum(at, 0)]

    each(0, 4 * KC, begin)
    multiply(1, lists, counts, cut, s_cut, c)
    c_copy = pltpu.make_async_copy(c, c_out, sems.at[8])
    c_copy.start()
    for copy in (cut_copy, s_copy, sp_copy, c_copy):
        copy.wait()


def far_kernel(final, lists, counts, below, above, left_in, sp_in, c_in, *refs):
    if final:
        out, stage, left, right, sp, s_cut, c, sems = refs
    else:
        sp_out, out, stage, left, right, sp, s_cut, c, sems = refs
    which = 4 if final else 2
    loads = [
        pltpu.make_async_copy(below, stage.at[pl.ds(0, PIECE)], sems.at[0]),
        pltpu.make_async_copy(above, stage.at[pl.ds(PIECE, PIECE)], sems.at[1]),
    ]
    ranges = ((0, 2 * KP), (10 * KP, 2 * KP + 1)) if final else ((0, 4 * KP), (8 * KP, 4 * KP + 1))
    for i, (at, n) in enumerate(ranges + ((4 * KP, 4 * KP),)):
        loads.append(pltpu.make_async_copy(left_in.at[pl.ds(at, n)], left.at[pl.ds(at, n)], sems.at[2 + i]))
    own_left = loads.pop()
    loads.append(pltpu.make_async_copy(sp_in, sp, sems.at[5]))
    c_copy = pltpu.make_async_copy(c_in, c, sems.at[6])
    for copy in loads + [own_left, c_copy]:
        copy.start()
    zero(right, 2 * PIECE)
    zero(s_cut, 4 * KS)
    for i, copy in enumerate(loads[:2]):
        copy.wait()
        each(i * PIECE, (i + 1) * PIECE, lambda q: put(right, q, stage[q]))
    for copy in loads[2:]:
        copy.wait()
    multiply(which, lists, counts, left, right, sp)
    done = []
    if not final:
        done.append(pltpu.make_async_copy(sp.at[pl.ds(4 * KS, 4 * KS)], sp_out, sems.at[7]))
        done[-1].start()
    each(0, 4 * KS, lambda q: put(s_cut, q, sp[q]))
    own_left.wait()
    c_copy.wait()
    multiply(which + 1, lists, counts, left, s_cut, c, scale=-2.0 if final else None)
    for i in range(ROWS):
        if not final:

            def finish(q):
                c[q] = -2.0 * c[q]

            each(i * KC, (i + 1) * KC, finish)
        piece = pl.ds(i * KC, KC)
        done.append(pltpu.make_async_copy(c.at[piece], out.at[piece], sems.at[8 + i]))
        done[-1].start()
    for copy in done:
        copy.wait()


SMEM = pl.BlockSpec(memory_space=pltpu.SMEM)
ANY = pl.BlockSpec(memory_space=pl.ANY)
VMEM = pl.BlockSpec(memory_space=pltpu.VMEM)


def f32(n):
    return jax.ShapeDtypeStruct((n, BS, BS), jnp.float32)


def vmem_cut(n):
    return pltpu.VMEM((n + 1, BS, 2 * BS), jnp.bfloat16)


def vmem_f32(n):
    return pltpu.VMEM((n, BS, BS), jnp.float32)


def near_step(lists, counts, carry, pieces):
    return pl.pallas_call(
        near_kernel,
        out_shape=(
            f32(4 * KS),
            f32(8 * KS),
            f32(4 * KC),
            jax.ShapeDtypeStruct((ZERO_LEFT + 1, BS, 2 * BS), jnp.bfloat16),
        ),
        in_specs=[SMEM] * 3 + [ANY] * 5,
        out_specs=(ANY,) * 4,
        scratch_shapes=[
            vmem_f32(12 * KP),
            vmem_cut(ZERO_LEFT),
            vmem_f32(12 * KS),
            vmem_cut(4 * KS),
            vmem_f32(4 * KC),
            pltpu.SemaphoreType.DMA((9,)),
        ],
        compiler_params=pltpu.CompilerParams(vmem_limit_bytes=48 * 1024 * 1024),
        cost_estimate=pl.CostEstimate(flops=20_000_000_000, bytes_accessed=60_000_000, transcendentals=0),
        name="near_step",
    )(lists, counts, carry, *pieces)


def far_step(final, lists, counts, below, above, left, sp, c):
    return pl.pallas_call(
        functools.partial(far_kernel, final),
        out_shape=f32(4 * KC) if final else (f32(4 * KS), f32(4 * KC)),
        in_specs=[SMEM] * 2 + [ANY] * 5,
        out_specs=ANY if final else (ANY, ANY),
        scratch_shapes=[
            vmem_f32(2 * PIECE),
            vmem_cut(ZERO_LEFT),
            vmem_cut(2 * PIECE),
            vmem_f32((4 if final else 8) * KS),
            vmem_cut(4 * KS),
            vmem_f32(4 * KC),
            pltpu.SemaphoreType.DMA((12,)),
        ],
        compiler_params=pltpu.CompilerParams(vmem_limit_bytes=36 * 1024 * 1024),
        cost_estimate=pl.CostEstimate(flops=10_000_000_000, bytes_accessed=40_000_000, transcendentals=0),
        name="last_step" if final else "middle_step",
    )(lists, counts, below, above, left, sp, c)


def split_kernel(src, one, two, sems):
    copies = [
        pltpu.make_async_copy(src.at[pl.ds(i * PIECE, PIECE)], dst, sems.at[i]) for i, dst in enumerate((one, two))
    ]
    for copy in copies:
        copy.start()
    for copy in copies:
        copy.wait()


def split(blocks):
    return pl.pallas_call(
        split_kernel,
        out_shape=(vmem_f32(PIECE), vmem_f32(PIECE)),
        in_specs=[ANY],
        out_specs=(VMEM, VMEM),
        scratch_shapes=[pltpu.SemaphoreType.DMA((2,))],
        cost_estimate=pl.CostEstimate(flops=0, bytes_accessed=4_000_000, transcendentals=0),
        name="split",
    )(blocks)


def local(density, pattern, square_target, cube_target):
    total_rows = ROWS * lax.axis_size(AXES)
    first_row = lax.axis_index(AXES) * ROWS
    base = jnp.remainder(first_row - 2 * ROWS, total_rows).astype(jnp.int32)
    hold = lax.optimization_barrier

    cols = jnp.concatenate([pattern, square_target], axis=1)
    cols_from = [shifted(cols, d) for d in (2, 1, -1, -2)]
    own = density.reshape(2 * PIECE, BS, BS)
    lower, upper = split(own)
    a1, a2 = shifted(upper, 1), shifted(lower, -1)
    lower, upper, pattern, square_target, cube_target, *cols_from = hold(
        (lower, upper, pattern, square_target, cube_target, *cols_from)
    )
    b1, b2 = shifted(lower, 1), shifted(upper, -1)
    near = jnp.concatenate(cols_from[:2] + [jnp.concatenate([pattern, square_target], axis=1)] + cols_from[2:], axis=0)
    table, hits, carry = pair_tables(base, near[:, :KP], near[4:16, KP:], cube_target, total_rows)
    a1, a2, table, hits, carry = hold((a1, a2, table, hits, carry))
    c1, c2 = shifted(a1, 1), shifted(a2, -1)
    lists, counts = pair_lists(table, hits)
    b1, b2, lists, counts, carry = hold((b1, b2, lists, counts, carry))
    d1, d2 = shifted(b1, 1), shifted(b2, -1)

    s_own, sp, c, left = near_step(lists, counts, carry, (b1, a1, own, a2, b2))
    sp, c = far_step(False, lists, counts, c1, c2, left, sp, c)
    out = far_step(True, lists, counts, d1, d2, left, sp, c)
    return s_own.reshape(ROWS, KS, BS, BS), out.reshape(ROWS, KC, BS, BS)


def solution(mesh):
    in_specs = (P(AXES, None, None, None), P(AXES, None), P(AXES, None), P(AXES, None))
    out_specs = (P(AXES, None, None, None), P(AXES, None, None, None))
    return jax.shard_map(local, mesh=mesh, in_specs=in_specs, out_specs=out_specs, check_vma=False)
```

```python
import functools

import jax
import jax.numpy as jnp
import numpy as np
from jax import lax
from jax.experimental import pallas as pl
from jax.experimental.pallas import tpu as pltpu
from jax.sharding import PartitionSpec as P

AXES = ("row", "col")
ROWS, KP, KS, KC, BS = 4, 8, 16, 24, 128
BLOCKS = ROWS * KP
PIECE = BLOCKS // 2
FIRST = PIECE + 4
SECOND = BLOCKS - FIRST
GROUP = 16
ZERO_LEFT = 12 * KP

OWN, MIDDLE, LAST = (4, 5, 6, 7), (2, 3, 8, 9), (0, 1, 10, 11)
ORDER = OWN + MIDDLE + LAST

TARGETS = (12 * KS, 4 * KC, 8 * KS, 4 * KC, 4 * KS, 4 * KC)
ZERO_RIGHT = (12 * KP, 4 * KS, 2 * PIECE, 4 * KS, 2 * PIECE, 4 * KS)
TABLE_OFF = tuple(int(x) for x in np.cumsum((0,) + tuple(t * KP for t in TARGETS)))
LIST_OFF = tuple(int(x) for x in np.cumsum((0,) + tuple(t * KP + GROUP for t in TARGETS)))


def shifted(x, distance):
    n = lax.axis_size(AXES)
    return lax.ppermute(x, AXES, [((i - distance) % n, i) for i in range(n)])


def lookup(rows, count):
    table = np.full((count,), -1, np.int32)
    table[list(rows)] = np.arange(len(rows))
    return table


def pair_tables(base, pat20, sq12, cu4, total_rows):
    def place(cols, start, count):
        return jnp.minimum(jnp.remainder(cols - start, total_rows), count - 1)

    def matched(left_cols, right_cols, targets):
        same = right_cols[:, None, :, :] == targets[:, :, None, None]
        same = same & (targets >= 0)[:, :, None, None] & (left_cols >= 0)[:, None, :, None]
        return jnp.max(jnp.where(same, jnp.arange(right_cols.shape[-1], dtype=jnp.int32), -1), axis=-1)

    def pick(table, index):
        hot = index[..., None] == jnp.arange(table.shape[0], dtype=jnp.int32)
        shape = hot.shape + (1,) * (table.ndim - 1)
        return jnp.sum(jnp.where(hot.reshape(shape), table, 0), axis=index.ndim)

    def entries(u, left, right_row, width, target):
        right = right_row[:, None, :] * width + u
        ok = (u >= 0) & (right_row >= 0)[:, None, :]
        return jnp.where(ok, left[:, None, :] | (right << 8) | (target[:, :, None] << 16), -1).reshape(-1, KP)

    def const(x):
        return jnp.asarray(np.asarray(x, np.int32))

    slots = np.arange(KP, dtype=np.int32)
    near_p = lookup(range(4, 16), 20)
    mid_p = lookup((2, 3, 16, 17), 20)
    last_p = lookup((0, 1, 18, 19), 20)

    pk = pat20[4:16]
    at = place(pk, base, 20)
    u = matched(pk, pick(pat20, at), sq12)
    pi = pat20[8:12]
    pi_at = place(pi, base + 4, 12)
    in_pattern = jnp.any((pi_at[:, :, None] == const(np.arange(12))) & (pi >= 0)[:, :, None], axis=1)
    in_cube = jnp.any(sq12[None, :, :, None] == cu4[:, None, None, :], axis=-1)
    used = jnp.any(in_pattern[:, :, None] & in_cube, axis=0) | const(lookup(OWN, 12) >= 0).astype(bool)[:, None]
    u = jnp.where(used[:, :, None], u, -1)
    tables = {}
    for which, (rows, here) in enumerate(((ORDER, near_p), (MIDDLE + LAST, mid_p), (LAST, last_p))):
        sel = np.asarray(rows)
        target = const(np.arange(len(rows))[:, None] * KS + np.arange(KS))
        take = lambda x: jnp.stack([x[r] for r in rows])
        tables[2 * which] = entries(take(u), const(np.arange(12)[sel][:, None] * KP + slots), pick(const(here), take(at)), KP, target)

    at = pi_at
    u = matched(pi, pick(sq12, at), cu4)
    left = const((np.arange(4) + 4)[:, None] * KP + slots)
    target = const(np.arange(4)[:, None] * KC + np.arange(KC))
    for which, rows in enumerate((OWN, MIDDLE, LAST)):
        tables[2 * which + 1] = entries(u, left, pick(const(lookup(rows, 12)), at), KS, target)

    same = (cu4[:, :, None] == sq12[4:8][:, None, :]) & (cu4 >= 0)[:, :, None]
    slot = jnp.max(jnp.where(same, jnp.arange(KS, dtype=jnp.int32), -1), axis=-1)
    carry = jnp.where(slot >= 0, slot + const(np.arange(4)[:, None] * KS), -1).reshape(-1)
    table = jnp.concatenate([tables[i] for i in range(6)])
    hit = table >= 0
    rank = jnp.sum(jnp.where(hit[:, None, :] & (slots[None, :] < slots[:, None])[None], 1, 0), axis=-1)
    moved = hit[:, None, :] & (rank[:, None, :] == slots[None, :, None])
    packed = jnp.sum(jnp.where(moved, table[:, None, :], 0), axis=-1)
    return packed.reshape(-1), jnp.sum(hit.astype(jnp.int32), axis=-1), carry


def list_kernel(table, hits, lists, counts):
    start = 0
    for which in range(6):
        t0, l0 = TABLE_OFF[which], LIST_OFF[which]

        def targets(i, n):
            first = i * 4
            h = [hits[start + first + q] for q in range(4)]
            at = [n]
            for q in range(4):
                at.append(at[-1] + h[q])
            e = [[table[t0 + (first + q) * KP + s] for s in range(4)] for q in range(4)]
            for q in range(4):
                for s in range(4):
                    lists[l0 + at[q] + s] = e[q][s]

                @pl.when(h[q] > 4)
                def _():
                    for s in range(4, KP):
                        lists[l0 + at[q] + s] = table[t0 + (first + q) * KP + s]

            return at[4]

        n = lax.fori_loop(0, TARGETS[which] // 4, targets, jnp.int32(0))
        start += TARGETS[which]
        filler = ZERO_LEFT | (ZERO_RIGHT[which] << 8)
        for q in range(GROUP):
            lists[l0 + n + q] = filler
        counts[which] = (n + GROUP - 1) // GROUP


def pair_lists(table, hits):
    smem = pl.BlockSpec(memory_space=pltpu.SMEM)
    return pl.pallas_call(
        list_kernel,
        out_shape=(
            jax.ShapeDtypeStruct((LIST_OFF[-1],), jnp.int32),
            jax.ShapeDtypeStruct((6,), jnp.int32),
        ),
        in_specs=[smem, smem],
        out_specs=(smem, smem),
        cost_estimate=pl.CostEstimate(flops=20_000_000, bytes_accessed=40_000_000, transcendentals=0),
        name="pair_lists",
    )(table, hits)


def halves(x):
    hi = x.astype(jnp.bfloat16)
    lo = (x - hi.astype(jnp.float32)).astype(jnp.bfloat16)
    return hi, lo


def put(ref, at, x):
    hi, lo = halves(x)
    ref[at, :, 0:BS] = hi
    ref[at, :, BS : 2 * BS] = lo


def each(lo, hi, body, step=4):
    def many(i, _):
        for q in range(step):
            body(lo + i * step + q)
        return 0

    lax.fori_loop(0, (hi - lo) // step, many, 0)


def multiply(which, lists, counts, left, right, total, scale=None):
    def group(g, _):
        at = LIST_OFF[which] + g * GROUP
        none = jnp.zeros((BS, BS), jnp.bfloat16)
        done = []
        for x in range(GROUP):
            e = lists[at + x]
            b = right[(e >> 8) & 255]
            rhs = jnp.concatenate([b, jnp.concatenate([b[:, :BS], none], axis=1)], axis=0)
            r = jnp.dot(left[e & 255], rhs, preferred_element_type=jnp.float32)
            done.append((e >> 16, r[:, :BS] + r[:, BS:]))
        for t, q in done:
            total[t] = total[t] + (q if scale is None else scale * q)
        return 0

    lax.fori_loop(0, counts[which], group, 0)


def zero(ref, at):
    ref[at] = jnp.zeros((BS, 2 * BS), jnp.bfloat16)


def near_kernel(lists, counts, carry, b1, a1, own, a2, b2, s_out, sp_out, c_out, cut_out, stage, cut, total, s_cut, c, sems):
    loads = []
    for i, (src, at, n) in enumerate(
        (
            (own, BLOCKS, BLOCKS),
            (a1, SECOND, FIRST),
            (a2, 2 * BLOCKS, FIRST),
            (b1, 0, SECOND),
            (b2, 2 * BLOCKS + FIRST, SECOND),
        )
    ):
        loads.append((pltpu.make_async_copy(src, stage.at[pl.ds(at, n)], sems.at[i]), at, n))
    for copy, _, _ in loads:
        copy.start()
    zero(cut, ZERO_LEFT)
    zero(s_cut, 4 * KS)

    def clear(q):
        total[q] = jnp.zeros((BS, BS), jnp.float32)

    each(0, 12 * KS, clear)
    for copy, at, n in loads:
        copy.wait()
        each(at, at + n, lambda q: put(cut, q, stage[q]))
    cut_copy = pltpu.make_async_copy(cut, cut_out, sems.at[5])
    cut_copy.start()
    multiply(0, lists, counts, cut, cut, total)
    s_copy = pltpu.make_async_copy(total.at[pl.ds(0, 4 * KS)], s_out, sems.at[6])
    sp_copy = pltpu.make_async_copy(total.at[pl.ds(4 * KS, 8 * KS)], sp_out, sems.at[7])
    s_copy.start()
    sp_copy.start()
    each(0, 4 * KS, lambda q: put(s_cut, q, total[q]))

    def begin(q):
        at = carry[q]
        kept = jnp.where(at >= 0, -1.5, 0.0)
        c[q] = kept * total[jnp.maximum(at, 0)]

    each(0, 4 * KC, begin)
    multiply(1, lists, counts, cut, s_cut, c)
    c_copy = pltpu.make_async_copy(c, c_out, sems.at[8])
    c_copy.start()
    for copy in (cut_copy, s_copy, sp_copy, c_copy):
        copy.wait()


def far_kernel(final, lists, counts, below, above, left_in, sp_in, c_in, *refs):
    if final:
        more_below, more_above, out, stage, left, right, sp, s_cut, c, sems = refs
    else:
        sp_out, out, stage, left, right, sp, s_cut, c, sems = refs
    which = 4 if final else 2
    extra = FIRST - PIECE
    if final:
        pieces = (
            (below, 0, 0, SECOND),
            (more_below, 0, SECOND, extra),
            (more_above, PIECE, PIECE, extra),
            (above, 0, PIECE + extra, SECOND),
        )
    else:
        pieces = ((below, extra, 0, PIECE), (above, 0, PIECE, PIECE))
    loads = []
    for i, (src, at, to, n) in enumerate(pieces):
        loads.append(pltpu.make_async_copy(src.at[pl.ds(at, n)], stage.at[pl.ds(to, n)], sems.at[12 + i]))
    ranges = ((0, 2 * KP), (10 * KP, 2 * KP + 1)) if final else ((0, 4 * KP), (8 * KP, 4 * KP + 1))
    for i, (at, n) in enumerate(ranges + ((4 * KP, 4 * KP),)):
        loads.append(pltpu.make_async_copy(left_in.at[pl.ds(at, n)], left.at[pl.ds(at, n)], sems.at[2 + i]))
    own_left = loads.pop()
    loads.append(pltpu.make_async_copy(sp_in, sp, sems.at[5]))
    c_copy = pltpu.make_async_copy(c_in, c, sems.at[6])
    for copy in loads + [own_left, c_copy]:
        copy.start()
    zero(right, 2 * PIECE)
    zero(s_cut, 4 * KS)
    for copy, (_, _, to, n) in zip(loads, pieces):
        copy.wait()
        each(to, to + n, lambda q: put(right, q, stage[q]))
    for copy in loads[len(pieces) :]:
        copy.wait()
    multiply(which, lists, counts, left, right, sp)
    done = []
    if not final:
        done.append(pltpu.make_async_copy(sp.at[pl.ds(4 * KS, 4 * KS)], sp_out, sems.at[7]))
        done[-1].start()
    each(0, 4 * KS, lambda q: put(s_cut, q, sp[q]))
    own_left.wait()
    c_copy.wait()
    multiply(which + 1, lists, counts, left, s_cut, c, scale=-2.0 if final else None)
    for i in range(ROWS):
        if not final:

            def finish(q):
                c[q] = -2.0 * c[q]

            each(i * KC, (i + 1) * KC, finish)
        piece = pl.ds(i * KC, KC)
        done.append(pltpu.make_async_copy(c.at[piece], out.at[piece], sems.at[8 + i]))
        done[-1].start()
    for copy in done:
        copy.wait()


SMEM = pl.BlockSpec(memory_space=pltpu.SMEM)
ANY = pl.BlockSpec(memory_space=pl.ANY)


def f32(n):
    return jax.ShapeDtypeStruct((n, BS, BS), jnp.float32)


def vmem_cut(n):
    return pltpu.VMEM((n + 1, BS, 2 * BS), jnp.bfloat16)


def vmem_f32(n):
    return pltpu.VMEM((n, BS, BS), jnp.float32)


def near_step(lists, counts, carry, pieces):
    return pl.pallas_call(
        near_kernel,
        out_shape=(
            f32(4 * KS),
            f32(8 * KS),
            f32(4 * KC),
            jax.ShapeDtypeStruct((ZERO_LEFT + 1, BS, 2 * BS), jnp.bfloat16),
        ),
        in_specs=[SMEM] * 3 + [ANY] * 5,
        out_specs=(ANY,) * 4,
        scratch_shapes=[
            vmem_f32(12 * KP),
            vmem_cut(ZERO_LEFT),
            vmem_f32(12 * KS),
            vmem_cut(4 * KS),
            vmem_f32(4 * KC),
            pltpu.SemaphoreType.DMA((9,)),
        ],
        compiler_params=pltpu.CompilerParams(vmem_limit_bytes=48 * 1024 * 1024),
        cost_estimate=pl.CostEstimate(flops=10_000_000_000, bytes_accessed=30_000_000, transcendentals=0),
        name="near_step",
    )(lists, counts, carry, *pieces)


def far_step(final, lists, counts, below, above, left, sp, c, *more):
    return pl.pallas_call(
        functools.partial(far_kernel, final),
        out_shape=f32(4 * KC) if final else (f32(4 * KS), f32(4 * KC)),
        in_specs=[SMEM] * 2 + [ANY] * (5 + len(more)),
        out_specs=ANY if final else (ANY, ANY),
        scratch_shapes=[
            vmem_f32(2 * PIECE),
            vmem_cut(ZERO_LEFT),
            vmem_cut(2 * PIECE),
            vmem_f32((4 if final else 8) * KS),
            vmem_cut(4 * KS),
            vmem_f32(4 * KC),
            pltpu.SemaphoreType.DMA((16,)),
        ],
        compiler_params=pltpu.CompilerParams(vmem_limit_bytes=36 * 1024 * 1024),
        cost_estimate=pl.CostEstimate(flops=10_000_000_000, bytes_accessed=40_000_000, transcendentals=0),
        name="last_step" if final else "middle_step",
    )(lists, counts, below, above, left, sp, c, *more)


def split_kernel(ranges, src, one, two, stage, sems):
    loads, stores, to = [], [], 0
    for i, ((at, n), dst) in enumerate(zip(ranges, (one, two))):
        for q in range(2):
            half = n // 2
            piece, k = stage.at[pl.ds(to, half)], 2 * i + q
            loads.append(pltpu.make_async_copy(src.at[pl.ds(at + q * half, half)], piece, sems.at[k]))
            stores.append(pltpu.make_async_copy(piece, dst.at[pl.ds(q * half, half)], sems.at[4 + k]))
            to += half
    for copy in loads:
        copy.start()
    for load, store in zip(loads, stores):
        load.wait()
        store.start()
    for copy in stores:
        copy.wait()


def split(blocks, *ranges):
    return pl.pallas_call(
        functools.partial(split_kernel, ranges),
        out_shape=tuple(f32(n) for _, n in ranges),
        in_specs=[ANY],
        out_specs=(ANY, ANY),
        scratch_shapes=[vmem_f32(sum(n for _, n in ranges)), pltpu.SemaphoreType.DMA((8,))],
        cost_estimate=pl.CostEstimate(flops=0, bytes_accessed=4_000_000, transcendentals=0),
        name="split",
    )(blocks)


def local(density, pattern, square_target, cube_target):
    total_rows = ROWS * lax.axis_size(AXES)
    first_row = lax.axis_index(AXES) * ROWS
    base = jnp.remainder(first_row - 2 * ROWS, total_rows).astype(jnp.int32)
    hold = lax.optimization_barrier

    cols = jnp.concatenate([pattern, square_target], axis=1)
    cols_from = [shifted(cols, d) for d in (2, 1, -1, -2)]
    own = density.reshape(BLOCKS, BS, BS)
    send_up, send_down = split(own, (SECOND, FIRST), (0, FIRST))
    a1, a2 = shifted(send_up, 1), shifted(send_down, -1)
    rest, pattern, square_target, cube_target, *cols_from = hold(
        (own, pattern, square_target, cube_target, *cols_from)
    )
    send_up, send_down = split(rest, (0, SECOND), (FIRST, SECOND))
    b1, b2 = shifted(send_up, 1), shifted(send_down, -1)
    near = jnp.concatenate(cols_from[:2] + [jnp.concatenate([pattern, square_target], axis=1)] + cols_from[2:], axis=0)
    table, hits, carry = pair_tables(base, near[:, :KP], near[4:16, KP:], cube_target, total_rows)
    a1, a2, table, hits, carry = hold((a1, a2, table, hits, carry))
    c1, c2 = shifted(a1, 1), shifted(a2, -1)
    lists, counts = pair_lists(table, hits)
    b1, b2, lists, counts, carry = hold((b1, b2, lists, counts, carry))
    d1, d2 = shifted(b1, 1), shifted(b2, -1)

    s_own, sp, c, left = near_step(lists, counts, carry, (b1, a1, own, a2, b2))
    sp, c = far_step(False, lists, counts, c1, c2, left, sp, c)
    out = far_step(True, lists, counts, d1, d2, left, sp, c, c1, c2)
    return s_own.reshape(ROWS, KS, BS, BS), out.reshape(ROWS, KC, BS, BS)


def solution(mesh):
    in_specs = (P(AXES, None, None, None), P(AXES, None), P(AXES, None), P(AXES, None))
    out_specs = (P(AXES, None, None, None), P(AXES, None, None, None))
    return jax.shard_map(local, mesh=mesh, in_specs=in_specs, out_specs=out_specs, check_vma=False)
```

```python
import functools

import jax
import jax.numpy as jnp
import numpy as np
from jax import lax
from jax.experimental import pallas as pl
from jax.experimental.pallas import tpu as pltpu
from jax.sharding import PartitionSpec as P

AXES = ("row", "col")
ROWS, KP, KS, KC, BS = 4, 8, 16, 24, 128
BLOCKS = ROWS * KP
PIECE = BLOCKS // 2
FIRST = PIECE + 4
SECOND = BLOCKS - FIRST
GROUP = 16
ZERO_LEFT = 12 * KP

OWN, MIDDLE, LAST = (4, 5, 6, 7), (2, 3, 8, 9), (0, 1, 10, 11)
ORDER = OWN + MIDDLE + LAST

TARGETS = (12 * KS, 4 * KC, 8 * KS, 4 * KC, 4 * KS, 4 * KC)
ZERO_RIGHT = (12 * KP, 4 * KS, 2 * PIECE, 4 * KS, 2 * PIECE, 4 * KS)
SPARE = (0, 0, 0, 0, 0, 4 * KC)
TABLE_OFF = tuple(int(x) for x in np.cumsum((0,) + tuple(t * KP for t in TARGETS)))
LIST_OFF = tuple(int(x) for x in np.cumsum((0,) + tuple(t * KP + 2 * GROUP for t in TARGETS)))


def shifted(x, distance):
    n = lax.axis_size(AXES)
    return lax.ppermute(x, AXES, [((i - distance) % n, i) for i in range(n)])


def lookup(rows, count):
    table = np.full((count,), -1, np.int32)
    table[list(rows)] = np.arange(len(rows))
    return table


def pair_tables(base, pat20, sq12, cu4, total_rows):
    def place(cols, start, count):
        return jnp.minimum(jnp.remainder(cols - start, total_rows), count - 1)

    def matched(left_cols, right_cols, targets):
        same = right_cols[:, None, :, :] == targets[:, :, None, None]
        same = same & (targets >= 0)[:, :, None, None] & (left_cols >= 0)[:, None, :, None]
        return jnp.max(jnp.where(same, jnp.arange(right_cols.shape[-1], dtype=jnp.int32), -1), axis=-1)

    def pick(table, index):
        hot = index[..., None] == jnp.arange(table.shape[0], dtype=jnp.int32)
        shape = hot.shape + (1,) * (table.ndim - 1)
        return jnp.sum(jnp.where(hot.reshape(shape), table, 0), axis=index.ndim)

    def entries(u, left, right_row, width, target):
        right = right_row[:, None, :] * width + u
        ok = (u >= 0) & (right_row >= 0)[:, None, :]
        return jnp.where(ok, left[:, None, :] | (right << 8) | (target[:, :, None] << 16), -1).reshape(-1, KP)

    def const(x):
        return jnp.asarray(np.asarray(x, np.int32))

    slots = np.arange(KP, dtype=np.int32)
    near_p = lookup(range(4, 16), 20)
    mid_p = lookup((2, 3, 16, 17), 20)
    last_p = lookup((0, 1, 18, 19), 20)

    pk = pat20[4:16]
    at = place(pk, base, 20)
    u = matched(pk, pick(pat20, at), sq12)
    pi = pat20[8:12]
    pi_at = place(pi, base + 4, 12)
    in_pattern = jnp.any((pi_at[:, :, None] == const(np.arange(12))) & (pi >= 0)[:, :, None], axis=1)
    in_cube = jnp.any(sq12[None, :, :, None] == cu4[:, None, None, :], axis=-1)
    used = jnp.any(in_pattern[:, :, None] & in_cube, axis=0) | const(lookup(OWN, 12) >= 0).astype(bool)[:, None]
    u = jnp.where(used[:, :, None], u, -1)
    tables = {}
    for which, (rows, here) in enumerate(((ORDER, near_p), (MIDDLE + LAST, mid_p), (LAST, last_p))):
        sel = np.asarray(rows)
        target = const(np.arange(len(rows))[:, None] * KS + np.arange(KS))
        take = lambda x: jnp.stack([x[r] for r in rows])
        tables[2 * which] = entries(take(u), const(np.arange(12)[sel][:, None] * KP + slots), pick(const(here), take(at)), KP, target)

    at = pi_at
    u = matched(pi, pick(sq12, at), cu4)
    left = const((np.arange(4) + 4)[:, None] * KP + slots)
    target = const(np.arange(4)[:, None] * KC + np.arange(KC))
    for which, rows in enumerate((OWN, MIDDLE, LAST)):
        tables[2 * which + 1] = entries(u, left, pick(const(lookup(rows, 12)), at), KS, target)

    same = (cu4[:, :, None] == sq12[4:8][:, None, :]) & (cu4 >= 0)[:, :, None]
    slot = jnp.max(jnp.where(same, jnp.arange(KS, dtype=jnp.int32), -1), axis=-1)
    carry = jnp.where(slot >= 0, slot + const(np.arange(4)[:, None] * KS), -1).reshape(-1)
    table = jnp.concatenate([tables[i] for i in range(6)])
    hit = table >= 0
    rank = jnp.sum(jnp.where(hit[:, None, :] & (slots[None, :] < slots[:, None])[None], 1, 0), axis=-1)
    moved = hit[:, None, :] & (rank[:, None, :] == slots[None, :, None])
    packed = jnp.sum(jnp.where(moved, table[:, None, :], 0), axis=-1)
    return packed.reshape(-1), jnp.sum(hit.astype(jnp.int32), axis=-1), carry


def list_kernel(table, hits, lists, counts):
    start = 0
    for which in range(6):
        t0, l0 = TABLE_OFF[which], LIST_OFF[which]

        def targets(i, n):
            first = i * 4
            h = [hits[start + first + q] for q in range(4)]
            at = [n]
            for q in range(4):
                at.append(at[-1] + h[q])
            e = [[table[t0 + (first + q) * KP + s] for s in range(4)] for q in range(4)]
            for q in range(4):
                for s in range(4):
                    lists[l0 + at[q] + s] = e[q][s]

                @pl.when(h[q] > 4)
                def _():
                    for s in range(4, KP):
                        lists[l0 + at[q] + s] = table[t0 + (first + q) * KP + s]

            return at[4]

        n = lax.fori_loop(0, TARGETS[which] // 4, targets, jnp.int32(0))
        start += TARGETS[which]
        filler = ZERO_LEFT | (ZERO_RIGHT[which] << 8) | (SPARE[which] << 16)
        for q in range(GROUP):
            lists[l0 + n + q] = filler
        counts[which] = (n + GROUP - 1) // GROUP


def pair_lists(table, hits):
    smem = pl.BlockSpec(memory_space=pltpu.SMEM)
    return pl.pallas_call(
        list_kernel,
        out_shape=(
            jax.ShapeDtypeStruct((LIST_OFF[-1],), jnp.int32),
            jax.ShapeDtypeStruct((6,), jnp.int32),
        ),
        in_specs=[smem, smem],
        out_specs=(smem, smem),
        cost_estimate=pl.CostEstimate(flops=20_000_000, bytes_accessed=40_000_000, transcendentals=0),
        name="pair_lists",
    )(table, hits)


def halves(x):
    hi = x.astype(jnp.bfloat16)
    lo = (x - hi.astype(jnp.float32)).astype(jnp.bfloat16)
    return hi, lo


def put(ref, at, x):
    hi, lo = halves(x)
    ref[at, :, 0:BS] = hi
    ref[at, :, BS : 2 * BS] = lo


def each(lo, hi, body, step=4):
    def many(i, _):
        for q in range(step):
            body(lo + i * step + q)
        return 0

    lax.fori_loop(0, (hi - lo) // step, many, 0)


def multiply(which, lists, counts, left, right, total):
    def group(g, _):
        multiply_group(which, g, lists, left, right, total)
        return 0

    lax.fori_loop(0, counts[which], group, 0)


def multiply_group(which, g, lists, left, right, total):
    at = LIST_OFF[which] + g * GROUP
    none = jnp.zeros((BS, BS), jnp.bfloat16)
    done = []
    for x in range(GROUP):
        e = lists[at + x]
        b = right[(e >> 8) & 255]
        rhs = jnp.concatenate([b, jnp.concatenate([b[:, :BS], none], axis=1)], axis=0)
        r = jnp.dot(left[e & 255], rhs, preferred_element_type=jnp.float32)
        done.append((e >> 16, r[:, :BS] + r[:, BS:]))
    for t, q in done:
        total[t] = total[t] + q


def zero(ref, at):
    ref[at] = jnp.zeros((BS, 2 * BS), jnp.bfloat16)


def near_kernel(lists, counts, carry, b1, a1, own, a2, b2, s_out, sp_out, c_out, cut_out, stage, cut, total, s_cut, c, sems):
    loads = []
    for i, (src, at, n) in enumerate(
        (
            (own, BLOCKS, BLOCKS),
            (a1, SECOND, FIRST),
            (a2, 2 * BLOCKS, FIRST),
            (b1, 0, SECOND),
            (b2, 2 * BLOCKS + FIRST, SECOND),
        )
    ):
        loads.append((pltpu.make_async_copy(src, stage.at[pl.ds(at, n)], sems.at[i]), at, n))
    for copy, _, _ in loads:
        copy.start()
    zero(cut, ZERO_LEFT)
    zero(s_cut, 4 * KS)

    def clear(q):
        total[q] = jnp.zeros((BS, BS), jnp.float32)

    each(0, 12 * KS, clear)
    for copy, at, n in loads:
        copy.wait()
        each(at, at + n, lambda q: put(cut, q, stage[q]))
    cut_copy = pltpu.make_async_copy(cut, cut_out, sems.at[5])
    cut_copy.start()
    multiply(0, lists, counts, cut, cut, total)
    s_copy = pltpu.make_async_copy(total.at[pl.ds(0, 4 * KS)], s_out, sems.at[6])
    sp_copy = pltpu.make_async_copy(total.at[pl.ds(4 * KS, 8 * KS)], sp_out, sems.at[7])
    s_copy.start()
    sp_copy.start()
    each(0, 4 * KS, lambda q: put(s_cut, q, total[q]))

    def begin(q):
        at = carry[q]
        kept = jnp.where(at >= 0, -1.5, 0.0)
        c[q] = kept * total[jnp.maximum(at, 0)]

    each(0, 4 * KC, begin)
    multiply(1, lists, counts, cut, s_cut, c)
    c_copy = pltpu.make_async_copy(c, c_out, sems.at[8])
    c_copy.start()
    for copy in (cut_copy, s_copy, sp_copy, c_copy):
        copy.wait()


def far_kernel(final, lists, counts, below, above, left_in, sp_in, c_in, *refs):
    if final:
        more_below, more_above, out, stage, left, right, sp, s_cut, c, sems = refs
    else:
        sp_out, out, stage, left, right, sp, s_cut, c, sems = refs
    which = 4 if final else 2
    extra = FIRST - PIECE
    if final:
        pieces = (
            (below, 0, 0, SECOND),
            (more_below, 0, SECOND, extra),
            (more_above, PIECE, PIECE, extra),
            (above, 0, PIECE + extra, SECOND),
        )
    else:
        pieces = ((below, extra, 0, PIECE), (above, 0, PIECE, PIECE))
    loads = []
    for i, (src, at, to, n) in enumerate(pieces):
        loads.append(pltpu.make_async_copy(src.at[pl.ds(at, n)], stage.at[pl.ds(to, n)], sems.at[12 + i]))
    ranges = ((0, 2 * KP), (10 * KP, 2 * KP + 1)) if final else ((0, 4 * KP), (8 * KP, 4 * KP + 1))
    for i, (at, n) in enumerate(ranges + ((4 * KP, 4 * KP),)):
        loads.append(pltpu.make_async_copy(left_in.at[pl.ds(at, n)], left.at[pl.ds(at, n)], sems.at[2 + i]))
    own_left = loads.pop()
    loads.append(pltpu.make_async_copy(sp_in, sp, sems.at[5]))
    c_copy = pltpu.make_async_copy(c_in, c.at[pl.ds(0, 4 * KC)], sems.at[6])
    for copy in loads + [own_left, c_copy]:
        copy.start()
    zero(right, 2 * PIECE)
    zero(s_cut, 4 * KS)
    for copy, (_, _, to, n) in zip(loads, pieces):
        copy.wait()
        each(to, to + n, lambda q: put(right, q, stage[q]))
    for copy in loads[len(pieces) :]:
        copy.wait()
    multiply(which, lists, counts, left, right, sp)
    done = []
    if not final:
        done.append(pltpu.make_async_copy(sp.at[pl.ds(4 * KS, 4 * KS)], sp_out, sems.at[7]))
        done[-1].start()
    each(0, 4 * KS, lambda q: put(s_cut, q, sp[q]))
    own_left.wait()
    c_copy.wait()
    if final:

        def row_copy(i):
            piece = pl.ds(i * KC, KC)
            return pltpu.make_async_copy(c.at[piece], out.at[piece], sems.at[8 + i])

        def row(i, g):
            def here(g):
                first = lists[LIST_OFF[5] + jnp.minimum(g, counts[5]) * GROUP] >> 16
                return jnp.logical_and(g < counts[5], first < (i + 1) * KC)

            def step(g):
                multiply_group(5, g, lists, left, s_cut, c)
                return g + 1

            g = lax.while_loop(here, step, g)

            def finish(q):
                c[i * KC + q] = -2.0 * c[i * KC + q]

            each(0, KC, finish)
            row_copy(i).start()
            return g

        lax.fori_loop(0, ROWS, row, jnp.int32(0))
        for i in range(ROWS):
            row_copy(i).wait()
        return
    multiply(which + 1, lists, counts, left, s_cut, c)
    done.append(pltpu.make_async_copy(c.at[pl.ds(0, 4 * KC)], out, sems.at[8]))
    done[-1].start()
    for copy in done:
        copy.wait()


SMEM = pl.BlockSpec(memory_space=pltpu.SMEM)
ANY = pl.BlockSpec(memory_space=pl.ANY)


def f32(n):
    return jax.ShapeDtypeStruct((n, BS, BS), jnp.float32)


def vmem_cut(n):
    return pltpu.VMEM((n + 1, BS, 2 * BS), jnp.bfloat16)


def vmem_f32(n):
    return pltpu.VMEM((n, BS, BS), jnp.float32)


def near_step(lists, counts, carry, pieces):
    return pl.pallas_call(
        near_kernel,
        out_shape=(
            f32(4 * KS),
            f32(8 * KS),
            f32(4 * KC),
            jax.ShapeDtypeStruct((ZERO_LEFT + 1, BS, 2 * BS), jnp.bfloat16),
        ),
        in_specs=[SMEM] * 3 + [ANY] * 5,
        out_specs=(ANY,) * 4,
        scratch_shapes=[
            vmem_f32(12 * KP),
            vmem_cut(ZERO_LEFT),
            vmem_f32(12 * KS),
            vmem_cut(4 * KS),
            vmem_f32(4 * KC),
            pltpu.SemaphoreType.DMA((9,)),
        ],
        compiler_params=pltpu.CompilerParams(vmem_limit_bytes=48 * 1024 * 1024),
        cost_estimate=pl.CostEstimate(flops=10_000_000_000, bytes_accessed=30_000_000, transcendentals=0),
        name="near_step",
    )(lists, counts, carry, *pieces)


def far_step(final, lists, counts, below, above, left, sp, c, *more):
    return pl.pallas_call(
        functools.partial(far_kernel, final),
        out_shape=f32(4 * KC) if final else (f32(4 * KS), f32(4 * KC)),
        in_specs=[SMEM] * 2 + [ANY] * (5 + len(more)),
        out_specs=ANY if final else (ANY, ANY),
        scratch_shapes=[
            vmem_f32(2 * PIECE),
            vmem_cut(ZERO_LEFT),
            vmem_cut(2 * PIECE),
            vmem_f32((4 if final else 8) * KS),
            vmem_cut(4 * KS),
            vmem_f32(4 * KC + 1),
            pltpu.SemaphoreType.DMA((16,)),
        ],
        compiler_params=pltpu.CompilerParams(vmem_limit_bytes=36 * 1024 * 1024),
        cost_estimate=pl.CostEstimate(flops=10_000_000_000, bytes_accessed=40_000_000, transcendentals=0),
        name="last_step" if final else "middle_step",
    )(lists, counts, below, above, left, sp, c, *more)


def split_kernel(ranges, src, one, two, stage, sems):
    loads, stores, to = [], [], 0
    for i, ((at, n), dst) in enumerate(zip(ranges, (one, two))):
        for q in range(2):
            half = n // 2
            piece, k = stage.at[pl.ds(to, half)], 2 * i + q
            loads.append(pltpu.make_async_copy(src.at[pl.ds(at + q * half, half)], piece, sems.at[k]))
            stores.append(pltpu.make_async_copy(piece, dst.at[pl.ds(q * half, half)], sems.at[4 + k]))
            to += half
    for copy in loads:
        copy.start()
    for load, store in zip(loads, stores):
        load.wait()
        store.start()
    for copy in stores:
        copy.wait()


def split(blocks, *ranges):
    return pl.pallas_call(
        functools.partial(split_kernel, ranges),
        out_shape=tuple(f32(n) for _, n in ranges),
        in_specs=[ANY],
        out_specs=(ANY, ANY),
        scratch_shapes=[vmem_f32(sum(n for _, n in ranges)), pltpu.SemaphoreType.DMA((8,))],
        cost_estimate=pl.CostEstimate(flops=0, bytes_accessed=4_000_000, transcendentals=0),
        name="split",
    )(blocks)


def local(density, pattern, square_target, cube_target):
    total_rows = ROWS * lax.axis_size(AXES)
    first_row = lax.axis_index(AXES) * ROWS
    base = jnp.remainder(first_row - 2 * ROWS, total_rows).astype(jnp.int32)
    hold = lax.optimization_barrier

    cols = jnp.concatenate([pattern, square_target], axis=1)
    cols_from = [shifted(cols, d) for d in (2, 1, -1, -2)]
    own = density.reshape(BLOCKS, BS, BS)
    send_up, send_down = split(own, (SECOND, FIRST), (0, FIRST))
    a1, a2 = shifted(send_up, 1), shifted(send_down, -1)
    rest, pattern, square_target, cube_target, *cols_from = hold(
        (own, pattern, square_target, cube_target, *cols_from)
    )
    send_up, send_down = split(rest, (0, SECOND), (FIRST, SECOND))
    b1, b2 = shifted(send_up, 1), shifted(send_down, -1)
    near = jnp.concatenate(cols_from[:2] + [jnp.concatenate([pattern, square_target], axis=1)] + cols_from[2:], axis=0)
    table, hits, carry = pair_tables(base, near[:, :KP], near[4:16, KP:], cube_target, total_rows)
    a1, a2, table, hits, carry = hold((a1, a2, table, hits, carry))
    c1, c2 = shifted(a1, 1), shifted(a2, -1)
    lists, counts = pair_lists(table, hits)
    b1, b2, lists, counts, carry = hold((b1, b2, lists, counts, carry))
    d1, d2 = shifted(b1, 1), shifted(b2, -1)

    s_own, sp, c, left = near_step(lists, counts, carry, (b1, a1, own, a2, b2))
    sp, c = far_step(False, lists, counts, c1, c2, left, sp, c)
    out = far_step(True, lists, counts, d1, d2, left, sp, c, c1, c2)
    return s_own.reshape(ROWS, KS, BS, BS), out.reshape(ROWS, KC, BS, BS)


def solution(mesh):
    in_specs = (P(AXES, None, None, None), P(AXES, None), P(AXES, None), P(AXES, None))
    out_specs = (P(AXES, None, None, None), P(AXES, None, None, None))
    return jax.shard_map(local, mesh=mesh, in_specs=in_specs, out_specs=out_specs, check_vma=False)
```
